256 devices in a mesh: mp: 8 (over y, core), batch: 32 (over x, z).
Axes of the slice: x: 4, y: 4, z: 8, core: 2. Of those that a mesh axis runs over, the one named last changes fastest.
Arguments:
- features: bfloat16 [4096, 1536], P('batch'), may hold values from -6 to 6
- labels: bfloat16 [4096], P('batch'), may hold values from 0 to 1
- scenario_ids: int32 [4096, 1], P('batch'), may hold values from 0 to 31; in each aligned block of 128 rows (0 to 127, 128 to 255, ...) at most 16 rows name the same one
- tower_owner: int32 [32], replicated, may hold values from 0 to 31, each once
- gate_w: bfloat16 [1536, 4096], P('batch', 'mp'), may hold values from -0.15625 to 0.15625
- up_w: bfloat16 [1536, 4096], P('batch', 'mp'), may hold values from -0.15625 to 0.15625
- down_w: bfloat16 [4096, 4096], P('mp', 'batch'), may hold values from -0.09375 to 0.09375
- cross_w: bfloat16 [32, 4096, 4096], P('batch', None, 'mp'), may hold values from -0.09375 to 0.09375
- cross_b: bfloat16 [32, 4096], P('batch', 'mp'), may hold values from -3 to 3
- out_w: bfloat16 [32, 4096], P('batch', 'mp'), may hold values from -0.09375 to 0.09375
Outputs:
- grad_gate: float32 [1536, 4096], P('batch', 'mp')
- grad_up: float32 [1536, 4096], P('batch', 'mp')
- grad_down: float32 [4096, 4096], P('mp', 'batch')
- grad_cross: bfloat16 [32, 4096, 4096], P('batch', None, 'mp')
- grad_cross_b: float32 [32, 4096], P('batch', 'mp')
- grad_out_w: float32 [32, 4096], P('batch', 'mp')
The draws below stay inside these ranges and needn't reach their ends.
Inputs may be any that keep to these rules, and one draw needn't show every extreme that they name: `scenario_ids`: among the rows of one batch index no scenario appears more than 16 times. `tower_owner`: every tower slot holds exactly one scenario.
All inputs are finite; a program needn't handle non-finite values.
Results may differ from the reference program's by a relative error of at most 0.023.
Values may be sent and summed in bfloat16 or wider, within the bound.
No kernel may reach another device: no remote copies, remote signals or barrier semaphores. Data moves between devices by JAX's collectives and lax.ppermute only.
A program may use at most 128 MiB of HBM per device.

```python
import math
import jax
import jax.numpy as jnp
import numpy as np
from jax import lax

F = 1536
H = 4096
D = 4096
ROWS_DEV = 128
SCEN = 32
TOKENS = 4096
CAP = 16
SLOTS = 512
N_BATCH = 32


def steps_of(stream_key, shape, split, least, top_value):
    loudness, own = 1.0, jax.random.fold_in(stream_key, 6)
    for axis_at, shards_of in split:
        draws = jnp.exp(jax.random.uniform(jax.random.fold_in(own, axis_at), (shards_of,), jnp.float32, least / len(split), top_value / len(split)))
        loudness = loudness * jnp.repeat(draws, shape[axis_at] // shards_of).reshape([-1 if axis == axis_at else 1 for axis in range(len(shape))])
    return loudness


def assign_block(rng, own, number, rows, count, top, reach, skew):
    ranking = jax.random.permutation(rng, count)
    crowded, usual = load_shares(count, rows * top, reach, skew, True), load_shares(count, rows * top, reach, skew, False)
    places = jnp.arange(count)

    def named(sizes, rotation):
        used = int((sizes > 0).sum())
        fixed = max(1, used // 4)
        moved = fixed + (places - fixed + rotation * (used - fixed)) % max(1, count - fixed)
        return jnp.zeros((count,), jnp.int32).at[ranking[jnp.where(places < fixed, places, moved)]].set(jnp.asarray(sizes, jnp.int32))

    sizes = jnp.where(number % 4 == 0, named(crowded, number // 4), named(usual, number - number // 4 - 1))
    mixed = jax.random.permutation(jax.random.fold_in(own, 3), count)
    source_of, receiver = mixed[0:count // 2 * 2:2], mixed[1:count // 2 * 2:2]
    margin = jnp.minimum(sizes[source_of] - 1, reach - sizes[receiver]) // 2
    margin = jnp.where((source_of == ranking[0]) | (receiver == ranking[0]) | (sizes[receiver] == 0), 0, jnp.maximum(margin, 0))
    moved = jax.random.randint(jax.random.fold_in(own, 4), (count // 2,), 0, 1 << 20) % (margin + 1)
    sizes = sizes.at[source_of].add(-moved).at[receiver].add(moved)
    members = jnp.searchsorted(jnp.cumsum(sizes), jnp.arange(rows * top), side="right").astype(jnp.int32)
    listing = members.reshape(top, rows).T
    listing = listing[jax.random.permutation(jax.random.fold_in(own, 1), rows)]
    rotation = jax.random.randint(jax.random.fold_in(own, 2), (rows, 1), 0, top)
    return jnp.take_along_axis(listing, (jnp.arange(top)[None, :] + rotation) % top, axis=1)


def load_shares(count, total, reach, lean, full):
    loads = [(1 << 20) // math.isqrt(grade ** lean) + 1 for grade in range(1, count + 1)]
    largest = reach if full else min(reach, max(-(-total // count), total * loads[0] // sum(loads)))
    least = 1 if total - largest >= count - 1 else 0
    holding, surplus = [largest] + [least] * (count - 1), total - largest - least * (count - 1)
    while surplus > 0:
        movable = [i for i in range(1, count) if holding[i] < largest] or [i for i in range(1, count) if holding[i] < reach]
        pool, left = sum([loads[i] for i in movable]), surplus
        for i in movable:
            addition = min(reach - holding[i], max(1, left * loads[i] // pool), surplus)
            holding[i] = holding[i] + addition
            surplus = surplus - addition
    return np.array(holding)


def normal_values(stream_key, dims, scale, limit, split=(), kind=jnp.bfloat16):
    array = jax.random.normal(stream_key, dims, jnp.float32) * scale
    if len(split) > 0:
        array = steps_of(stream_key, dims, split, -0.22, 0.18) * array
    return jnp.clip(array, min=-limit, max=limit).astype(kind)


def setup_inputs(seed: int = 0) -> dict:
    streams_of = jax.random.split(jax.random.key(seed), 11)
    features = normal_values(streams_of[0], (TOKENS, F), 1.0, 6.0, ((0, 32),))
    labels = jnp.clip(1.0 * jax.random.uniform(streams_of[1], (TOKENS,), jnp.float32) ** steps_of(streams_of[1], (TOKENS,), ((0, 32),), -0.2, 0.2), 0.0, 1.0).astype(jnp.bfloat16)
    scenario_ids_keys = jax.random.split(jax.random.fold_in(streams_of[2], 1), TOKENS // ROWS_DEV)
    scenario_ids_turns = jax.random.permutation(jax.random.fold_in(streams_of[2], 3), TOKENS // ROWS_DEV)
    scenario_ids = jax.vmap(lambda own, number: assign_block(jax.random.fold_in(streams_of[2], 2), own, number, ROWS_DEV, SCEN, 1, CAP, 2))(scenario_ids_keys, scenario_ids_turns).reshape((TOKENS, 1))
    tower_owner = jax.random.permutation(streams_of[3], SCEN).astype(jnp.int32)
    gate_w = normal_values(streams_of[4], (F, H), F ** -0.5, 0.15625, ((0, 32), (1, 8)))
    up_w = normal_values(streams_of[5], (F, H), F ** -0.5, 0.15625, ((0, 32), (1, 8)))
    down_w = normal_values(streams_of[6], (H, D), H ** -0.5, 0.09375, ((0, 8), (1, 32)))
    cross_w = normal_values(streams_of[7], (SCEN, D, D), D ** -0.5, 0.09375, ((0, 32), (2, 8)))
    cross_b = normal_values(streams_of[8], (SCEN, D), 0.5, 3.0, ((0, 32), (1, 8)))
    out_w = normal_values(streams_of[9], (SCEN, D), D ** -0.5, 0.09375, ((0, 32), (1, 8)))
    return {"features": features, "labels": labels, "scenario_ids": scenario_ids, "tower_owner": tower_owner, "gate_w": gate_w, "up_w": up_w, "down_w": down_w, "cross_w": cross_w, "cross_b": cross_b, "out_w": out_w}


def slot_layout(scenario_ids, tower_owner):
    scenario = scenario_ids[:, 0]
    one_hot = (scenario[:, None] == jnp.arange(SCEN, dtype=jnp.int32)[None, :]).astype(jnp.int32)
    owner_of = jnp.sum(one_hot * tower_owner[None, :], axis=1).astype(jnp.int32)
    blocked = one_hot.reshape(N_BATCH, ROWS_DEV, SCEN)
    earlier = jnp.cumsum(blocked, axis=1) - blocked
    rank_in = jnp.sum(earlier * blocked, axis=2).reshape(TOKENS).astype(jnp.int32)
    source = (jnp.arange(TOKENS, dtype=jnp.int32) // ROWS_DEV).astype(jnp.int32)
    return owner_of, (source * CAP + rank_in).astype(jnp.int32)


def tower_step(inputs):
    tower_rows, tower_labels, weight, bias, out_vec = inputs
    pre_cross = jnp.dot(tower_rows, weight, preferred_element_type=jnp.float32)
    shifted = pre_cross + bias.astype(jnp.float32)[None, :]
    row_float = tower_rows.astype(jnp.float32)
    crossed = row_float * shifted + row_float
    out_float = out_vec.astype(jnp.float32)
    logit = jnp.sum(crossed * out_float[None, :], axis=1)
    d_logit = jax.nn.sigmoid(logit) - tower_labels
    grad_outvec = jnp.sum(d_logit[:, None] * crossed, axis=0)
    d_crossed = d_logit[:, None] * out_float[None, :]
    d_pre = d_crossed * row_float
    grad_bias = jnp.sum(d_pre, axis=0)
    d_pre_b = d_pre.astype(jnp.bfloat16)
    grad_weight = jnp.dot(tower_rows.T, d_pre_b, preferred_element_type=jnp.float32).astype(jnp.bfloat16)
    back_term = jnp.dot(d_pre_b, weight.T, preferred_element_type=jnp.float32)
    d_rows = (back_term + d_crossed * (shifted + 1.0)).astype(jnp.bfloat16)
    return d_rows, grad_weight, grad_bias, grad_outvec


def accumulate(carry, block):
    feat_block, dgate_block, dup_block, hidden_block, dtrunk_block = block
    gate_term = jnp.dot(feat_block.T, dgate_block, preferred_element_type=jnp.float32)
    up_term = jnp.dot(feat_block.T, dup_block, preferred_element_type=jnp.float32)
    down_term = jnp.dot(hidden_block.T, dtrunk_block, preferred_element_type=jnp.float32)
    rounded = lax.optimization_barrier((gate_term.astype(jnp.bfloat16), up_term.astype(jnp.bfloat16), down_term.astype(jnp.bfloat16)))
    new_carry = (carry[0] + rounded[0].astype(jnp.float32), carry[1] + rounded[1].astype(jnp.float32), carry[2] + rounded[2].astype(jnp.float32))
    return new_carry, None


def reference(features, labels, scenario_ids, tower_owner, gate_w, up_w, down_w, cross_w, cross_b, out_w):
    gate_pre = jnp.dot(features, gate_w, preferred_element_type=jnp.float32)
    up_pre = jnp.dot(features, up_w, preferred_element_type=jnp.float32)
    gate_sig = jax.nn.sigmoid(gate_pre)
    activated = gate_pre * gate_sig
    hidden = (activated * up_pre).astype(jnp.bfloat16)
    trunk_out = jnp.dot(hidden, down_w, preferred_element_type=jnp.float32).astype(jnp.bfloat16)
    owner_of, slot_of = slot_layout(scenario_ids, tower_owner)
    row_buffer = jnp.zeros((SCEN, SLOTS, D), jnp.bfloat16).at[owner_of, slot_of].set(trunk_out)
    label_buffer = jnp.zeros((SCEN, SLOTS), jnp.float32).at[owner_of, slot_of].set(labels.astype(jnp.float32))
    d_buffer, grad_cross, grad_cross_b, grad_out_w = lax.map(tower_step, (row_buffer, label_buffer, cross_w, cross_b, out_w))
    d_trunk = d_buffer[owner_of, slot_of]
    d_hidden = jnp.dot(d_trunk, down_w.T, preferred_element_type=jnp.float32)
    d_up = (d_hidden * activated).astype(jnp.bfloat16)
    d_gate = (d_hidden * up_pre * gate_sig * (1.0 + gate_pre * (1.0 - gate_sig))).astype(jnp.bfloat16)
    blocks = (features.reshape(N_BATCH, ROWS_DEV, F), d_gate.reshape(N_BATCH, ROWS_DEV, H), d_up.reshape(N_BATCH, ROWS_DEV, H), hidden.reshape(N_BATCH, ROWS_DEV, H), d_trunk.reshape(N_BATCH, ROWS_DEV, D))
    start_sums = (jnp.zeros((F, H), jnp.float32), jnp.zeros((F, H), jnp.float32), jnp.zeros((H, D), jnp.float32))
    totals, _ = lax.scan(accumulate, start_sums, blocks)
    return totals[0], totals[1], totals[2], grad_cross, grad_cross_b, grad_out_w
```

```python
import jax
import jax.numpy as jnp
from jax import lax
from jax.sharding import Mesh, PartitionSpec as P

BATCH = ("x", "z")
MP = ("y", "c")
BF = jnp.bfloat16
F32 = jnp.float32


def ring(value, axis):
    count = lax.axis_size(axis)
    return [value] + [
        lax.ppermute(value, axis, [(i, (i - s) % count) for i in range(count)])
        for s in range(1, count)
    ]


def turned(stacked, start):
    count = stacked.shape[0]
    return lax.dynamic_slice_in_dim(jnp.concatenate([stacked, stacked]), start, count)


def exchange(value, axes):
    return lax.all_to_all(value, axes, split_axis=0, concat_axis=0, tiled=True)


def pair(value):
    other = lax.ppermute(value, "c", [(0, 1), (1, 0)])
    first = lax.axis_index("c") == 0
    return jnp.where(first, value, other), jnp.where(first, other, value)


def dot(left, right, contract):
    return lax.dot_general(left, right, (contract, ((), ())), preferred_element_type=F32)


def per_device(
    features, labels, scenario_ids, tower_owner, gate_w, up_w, down_w, cross_w, cross_b, out_w
):
    nx, nz, ny = lax.axis_size("x"), lax.axis_size("z"), lax.axis_size("y")
    nb, nm = nx * nz, 2 * ny
    x, z, y, c = (lax.axis_index(name) for name in ("x", "z", "y", "c"))
    rows, depth = features.shape
    part = gate_w.shape[0]
    width = cross_w.shape[2]
    block = down_w.shape[1]
    cap = 4 * rows // nb
    group = nx * rows
    slots = nb * cap
    weight = cross_w[0]
    out_float = out_w[0].astype(F32)

    feats = jnp.concatenate(ring(features, "x"), axis=0)
    aux = jnp.concatenate(
        [
            scenario_ids.reshape(1, rows).astype(BF),
            labels.reshape(1, rows),
            jnp.zeros((6, rows), BF),
        ],
        axis=0,
    )
    by_x = lambda w: w.reshape(part, nx, block).transpose(1, 0, 2)
    packed = jnp.concatenate(
        [by_x(gate_w), by_x(up_w), jnp.broadcast_to(aux[None], (nx, 8, rows))], axis=1
    )
    packed = jnp.broadcast_to(packed[:, None], (nx, nz) + packed.shape[1:])
    got = exchange(packed.reshape((nb,) + packed.shape[2:]), BATCH)
    both_w = jnp.concatenate([got[:, :part], got[:, part : 2 * part]], axis=2)
    both_w = both_w.reshape(depth, 2 * block)
    ids_all = got[:, 2 * part].astype(jnp.int32)
    labels_all = got[:, 2 * part + 1].astype(F32)

    spread = [(b, b) for b in range(nb)]
    blocks = []
    for k in range(nm):
        perm = []
        for xi in range(nx):
            for zi in range(nz):
                perm.append((nx * ((zi + k) % nm) + xi, xi * nz + zi))
        blocks.append(lax.ppermute(down_w, BATCH, perm))
    down = turned(jnp.stack(blocks), (nm - z) % nm)

    scaled = (weight.astype(F32) * out_float[None, :]).astype(BF).reshape(ny, 2, width, width)
    mine = jnp.where(c == 0, scaled[:, 0], scaled[:, 1])
    theirs = jnp.where(c == 0, scaled[:, 1], scaled[:, 0])
    swapped = lax.ppermute(theirs, "c", [(0, 1), (1, 0)])
    halves = jnp.where(c == 0, jnp.concatenate([mine, swapped], axis=2), jnp.concatenate([swapped, mine], axis=2))
    back_w = []
    for s in range(ny):
        piece = lax.dynamic_index_in_dim(halves, (y - s) % ny, 0, False)
        if s:
            piece = lax.ppermute(piece, "y", [(i, (i - s) % ny) for i in range(ny)])
        back_w.append(piece)

    ids_group = lax.dynamic_index_in_dim(ids_all.reshape(nx, nz, rows), z, 1, False)
    labels_group = lax.dynamic_index_in_dim(labels_all.reshape(nx, nz, rows), z, 1, False)
    owner = jnp.sum(
        jnp.where(
            ids_group[:, :, None] == jnp.arange(tower_owner.shape[0], dtype=jnp.int32),
            tower_owner[None, None, :],
            0,
        ),
        axis=2,
    )
    place = jnp.arange(rows, dtype=jnp.int32)
    rank = jnp.sum(
        (
            (ids_group[:, :, None] == ids_group[:, None, :])
            & (place[None, :, None] > place[None, None, :])
        ).astype(jnp.int32),
        axis=2,
    )
    slot = owner * (nx * cap) + jnp.arange(nx, dtype=jnp.int32)[:, None] * cap + rank
    placing = (
        jnp.arange(nb * nx * cap, dtype=jnp.int32)[:, None] == slot.reshape(1, group)
    ).astype(BF)

    pre = dot(feats, both_w, ((1,), (0,)))
    pre = turned(pre.reshape(nx, rows, 2 * block), (nx - x) % nx).reshape(group, 2 * block)
    gate_pre, up_pre = pre[:, :block], pre[:, block:]
    gate_sig = jax.nn.sigmoid(gate_pre)
    activated = gate_pre * gate_sig
    hidden_own = (activated * up_pre).astype(BF)
    hidden = exchange(jnp.broadcast_to(hidden_own[None], (nx, group, block)), "x")
    hidden = hidden.transpose(1, 0, 2).reshape(group, nx * block)
    partial = jnp.einsum("rk,mkj->mrj", hidden, down, preferred_element_type=F32).astype(BF)
    trunk = jnp.sum(exchange(partial, MP).astype(F32), axis=0).astype(BF)

    outgoing = dot(placing, trunk, ((1,), (0,))).astype(BF)
    arrived = exchange(outgoing.reshape(nb, nx * cap, block), BATCH)
    tower_local = arrived.reshape(nx, slots, block).transpose(1, 0, 2).reshape(slots, width)
    tower = [jnp.concatenate(pair(piece), axis=1) for piece in ring(tower_local, "y")]

    weight_chips = weight.reshape(ny, 2 * width, width)
    pre_cross = 0.0
    back = 0.0
    for s in range(ny):
        rows_of = lax.dynamic_index_in_dim(weight_chips, (y + s) % ny, 0, False)
        pre_cross = pre_cross + dot(tower[s], rows_of, ((1,), (0,)))
        back = back + dot(tower[s], back_w[s], ((1,), (1,)))
    shifted = pre_cross + cross_b[0].astype(F32)[None, :]
    local_float = tower_local.astype(F32)
    crossed = local_float * shifted + local_float
    logit_part = jnp.sum(crossed * out_float[None, :], axis=1)
    unscaled = (back + out_float[None, :] * (shifted + 1.0)).astype(BF)

    part_by_z = logit_part.reshape(nz, nx * cap)
    high = part_by_z.astype(BF)
    low = (part_by_z - high.astype(F32)).astype(BF)
    tail = jnp.concatenate([high, low], axis=1)
    tail = jnp.concatenate([tail[:, None], jnp.zeros((nz, 7, block), BF)], axis=1)
    sent = unscaled.reshape(slots, nx, block).transpose(1, 0, 2).reshape(nx, nz, nx * cap, block)
    sent = jnp.concatenate([sent, jnp.broadcast_to(tail[None], (nx,) + tail.shape)], axis=2)
    returned = exchange(sent.reshape(nb, nx * cap + 8, block), BATCH)
    row_cols = dot(placing, returned[:, : nx * cap].reshape(nb * nx * cap, block), ((0,), (0,)))
    logits = returned[:, nx * cap].reshape(nb, 2, nx * cap).transpose(1, 0, 2)
    logits = dot(logits.reshape(2, nb * nx * cap), placing, ((1,), (0,)))
    mixed = jnp.concatenate(
        [row_cols.astype(BF), logits.astype(BF).reshape(2 * nx, block)], axis=0
    )
    mixed = jnp.stack(ring(mixed, "y"))
    mixed = turned(jnp.stack(pair(mixed), axis=1), (ny - y) % ny)
    mixed = mixed.reshape(nm, group + 2 * nx, block)
    logit_rows = jnp.sum(mixed[:, group:].astype(F32), axis=0)
    logit_rows = logit_rows[:nx] + logit_rows[nx:]
    d_logit_rows = (jax.nn.sigmoid(logit_rows) - labels_group).reshape(group)
    d_trunk = (mixed[:, :group].astype(F32) * d_logit_rows[None, :, None]).astype(BF)

    down_term = jnp.einsum("rk,mrj->mkj", hidden, d_trunk, preferred_element_type=F32).astype(BF)
    grad_down = 0.0
    for k in range(nm):
        perm = []
        for xi in range(nx):
            for zi in range(nz):
                perm.append((xi * nz + zi, nx * ((zi + k) % nm) + xi))
        piece = lax.dynamic_index_in_dim(down_term, (z + k) % nm, 0, False)
        grad_down = grad_down + lax.ppermute(piece, BATCH, perm).astype(F32)
    d_hidden = jnp.einsum("mrj,mkj->rk", d_trunk, down, preferred_element_type=F32).astype(BF)
    d_hidden = d_hidden.reshape(group, nx, block).transpose(1, 0, 2)
    d_hidden = jnp.sum(exchange(d_hidden, "x").astype(F32), axis=0)
    d_up = d_hidden * activated
    d_gate = d_hidden * up_pre * gate_sig * (1.0 + gate_pre * (1.0 - gate_sig))
    d_both = jnp.concatenate([d_gate, d_up], axis=1).astype(BF).reshape(nx, rows, 2 * block)
    d_both = turned(d_both, x).reshape(group, 2 * block)
    term = dot(feats, d_both, ((0,), (0,))).astype(BF)
    term = exchange(term.reshape(nb, part, 2 * block), BATCH)
    term = jnp.sum(term.reshape(nx, nz, part, 2 * block).astype(F32), axis=1)
    flat = lambda t: t.transpose(1, 0, 2).reshape(part, nx * block)
    grad_gate, grad_up = flat(term[:, :, :block]), flat(term[:, :, block:])

    at = lax.axis_index(BATCH)
    mask = jnp.sum(
        jnp.where(
            ids_all[:, :, None] == jnp.arange(tower_owner.shape[0], dtype=jnp.int32),
            tower_owner[None, None, :],
            0,
        ),
        axis=2,
    ) == at
    before = jnp.sum(
        (mask[:, None, :] & (place[None, :, None] > place[None, None, :])).astype(jnp.int32), axis=2
    )
    slot_labels = jnp.sum(
        jnp.where(
            mask[:, :, None] & (before[:, :, None] == jnp.arange(cap, dtype=jnp.int32)),
            labels_all[:, :, None],
            0.0,
        ),
        axis=1,
    )
    slot_labels = slot_labels.reshape(nx, nz, cap).transpose(1, 0, 2).reshape(slots)
    d_logit = jax.nn.sigmoid(lax.psum(logit_part, MP)) - slot_labels
    grad_outvec = jnp.sum(d_logit[:, None] * crossed, axis=0)
    d_pre = d_logit[:, None] * out_float[None, :] * local_float
    grad_bias = jnp.sum(d_pre, axis=0)
    d_pre_b = d_pre.astype(BF)
    grad_weight = jnp.stack([dot(piece, d_pre_b, ((0,), (0,))).astype(BF) for piece in tower])
    grad_weight = turned(grad_weight, (ny - y) % ny).reshape(1, nm * width, width)
    return (grad_gate, grad_up, grad_down, grad_weight, grad_bias[None], grad_outvec[None])


def solution(mesh):
    split = Mesh(mesh.devices.reshape(4, 2, 4, 8), ("y", "c", "x", "z"))
    placed = (
        P(BATCH, None),
        P(BATCH),
        P(BATCH, None),
        P(),
        P(BATCH, MP),
        P(BATCH, MP),
        P(MP, BATCH),
        P(BATCH, None, MP),
        P(BATCH, MP),
        P(BATCH, MP),
    )
    return jax.shard_map(
        per_device,
        mesh=split,
        in_specs=placed,
        out_specs=(
            P(BATCH, MP),
            P(BATCH, MP),
            P(MP, BATCH),
            P(BATCH, None, MP),
            P(BATCH, MP),
            P(BATCH, MP),
        ),
        check_vma=False,
    )
```

```python
import jax
import jax.numpy as jnp
from jax import lax
from jax.experimental import pallas as pl
from jax.experimental.pallas import tpu as pltpu
from jax.sharding import Mesh, PartitionSpec as P

BATCH = ("x", "z")
MP = ("y", "c")
BF = jnp.bfloat16
F32 = jnp.float32


def ring(value, axis):
    count = lax.axis_size(axis)
    return [value] + [
        lax.ppermute(value, axis, [(i, (i - s) % count) for i in range(count)])
        for s in range(1, count)
    ]


def turned(stacked, start):
    count = stacked.shape[0]
    return lax.dynamic_slice_in_dim(jnp.concatenate([stacked, stacked]), start, count)


def exchange(value, axes):
    return lax.all_to_all(value, axes, split_axis=0, concat_axis=0, tiled=True)


def pair(value):
    other = lax.ppermute(value, "c", [(0, 1), (1, 0)])
    first = lax.axis_index("c") == 0
    return jnp.where(first, value, other), jnp.where(first, other, value)


def dot(left, right, contract):
    return lax.dot_general(left, right, (contract, ((), ())), preferred_element_type=F32)


def shift(value, axis, places):
    count = lax.axis_size(axis)
    return lax.ppermute(value, axis, [(i, (i + places) % count) for i in range(count)])


def cross_body(whose, *refs):
    count = len(refs) - 10
    pieces = refs[:count]
    weight, back_own, back_other, bias, vector, crossed, unscaled, logit = refs[count : count + 8]
    pre_sum, back_sum = refs[count + 8 : count + 10]
    step = pl.program_id(0)

    @pl.when(step == 0)
    def _():
        pre_sum[...] = jnp.zeros_like(pre_sum)
        back_sum[...] = jnp.zeros_like(back_sum)

    for k in range(count):

        @pl.when(step == k)
        def _(k=k):
            piece = pieces[k][...]
            back = back_other if k % 2 else back_own
            pre_sum[...] += dot(piece, weight[0], ((1,), (0,)))
            back_sum[...] += dot(piece, back[0], ((1,), (1,)))

    @pl.when(step == count - 1)
    def _():
        own = pieces[0][...].astype(F32)
        by = vector[...].astype(F32)
        shifted = pre_sum[...] + bias[...].astype(F32)
        whole = own * shifted + own
        crossed[...] = whole
        logit[...] = jnp.sum(whole * by, axis=1, keepdims=True)
        result = (back_sum[...] + by * (shifted + 1.0)).astype(BF)
        for part in range(unscaled.shape[0]):
            lanes = unscaled.shape[2]
            unscaled[part] = result[:, part * lanes : (part + 1) * lanes]


def cross_layer(whose, pieces, weight, back_own, back_other, bias, vector, parts):
    count, slots, width = len(pieces), *pieces[0].shape
    whole = lambda shape: pl.BlockSpec(shape, lambda i, w: (0,) * len(shape))
    half = pl.BlockSpec((1, width, width), lambda i, w: (i // 2, 0, 0))
    return pl.pallas_call(
        cross_body,
        grid_spec=pltpu.PrefetchScalarGridSpec(
            num_scalar_prefetch=1,
            grid=(count,),
            in_specs=[whole((slots, width))] * count
            + [pl.BlockSpec((1, width, width), lambda i, w: (w[i], 0, 0)), half, half]
            + [whole((1, width))] * 2,
            out_specs=[
                whole((slots, width)),
                whole((parts, slots, width // parts)),
                whole((slots, 1)),
            ],
            scratch_shapes=[pltpu.VMEM((slots, width), F32)] * 2,
        ),
        out_shape=[
            jax.ShapeDtypeStruct((slots, width), F32),
            jax.ShapeDtypeStruct((parts, slots, width // parts), BF),
            jax.ShapeDtypeStruct((slots, 1), F32),
        ],
        compiler_params=pltpu.CompilerParams(vmem_limit_bytes=44 * 2**20),
        cost_estimate=pl.CostEstimate(
            flops=4 * count * slots * width * width,
            bytes_accessed=6 * count * width * width,
            transcendentals=0,
        ),
    )(whose, *pieces, weight, back_own, back_other, bias, vector)


def grad_body(whose, *refs):
    pieces, right, out = refs[:-2], refs[-2], refs[-1]
    step = pl.program_id(0)
    for k in range(len(pieces)):

        @pl.when(step == k)
        def _(k=k):
            out[0] = dot(pieces[k][...], right[...], ((0,), (0,))).astype(BF)


def cross_grad(whose, pieces, right):
    count, slots, width = len(pieces), *pieces[0].shape
    return pl.pallas_call(
        grad_body,
        grid_spec=pltpu.PrefetchScalarGridSpec(
            num_scalar_prefetch=1,
            grid=(count,),
            in_specs=[pl.BlockSpec((slots, width), lambda i, w: (0, 0))] * (count + 1),
            out_specs=pl.BlockSpec((1, width, width), lambda i, w: (w[i], 0, 0)),
        ),
        out_shape=jax.ShapeDtypeStruct((count, width, width), BF),
        compiler_params=pltpu.CompilerParams(vmem_limit_bytes=44 * 2**20),
        cost_estimate=pl.CostEstimate(
            flops=2 * count * slots * width * width,
            bytes_accessed=4 * count * width * width,
            transcendentals=0,
        ),
    )(whose, *pieces, right)


def per_device(
    features, labels, scenario_ids, tower_owner, gate_w, up_w, down_w, cross_w, cross_b, out_w
):
    nx, nz, ny = lax.axis_size("x"), lax.axis_size("z"), lax.axis_size("y")
    nb, nm = nx * nz, 2 * ny
    x, z, y, c = (lax.axis_index(name) for name in ("x", "z", "y", "c"))
    rows, depth = features.shape
    part = gate_w.shape[0]
    width = cross_w.shape[2]
    block = down_w.shape[1]
    cap = 4 * rows // nb
    group = nx * rows
    slots = nb * cap
    weight = cross_w[0]
    out_float = out_w[0].astype(F32)

    feats = jnp.concatenate(ring(features, "x"), axis=0)
    aux = jnp.concatenate(
        [
            scenario_ids.reshape(1, rows).astype(BF),
            labels.reshape(1, rows),
            jnp.zeros((6, rows), BF),
        ],
        axis=0,
    )
    by_x = lambda w: w.reshape(part, nx, block).transpose(1, 0, 2)
    packed = jnp.concatenate(
        [by_x(gate_w), by_x(up_w), jnp.broadcast_to(aux[None], (nx, 8, rows))], axis=1
    )
    packed = jnp.broadcast_to(packed[:, None], (nx, nz) + packed.shape[1:])
    got = exchange(packed.reshape((nb,) + packed.shape[2:]), BATCH)
    both_w = jnp.concatenate([got[:, :part], got[:, part : 2 * part]], axis=2)
    both_w = both_w.reshape(depth, 2 * block)
    ids_all = got[:, 2 * part].astype(jnp.int32)
    labels_all = got[:, 2 * part + 1].astype(F32)

    spread = [(nx * m + i, i * nz + m) for m in range(nm) for i in range(nx)]
    turned_down = turned(down_w.reshape(nx, block, block), lax.axis_index(BATCH) % nx)
    down = lax.ppermute(turned_down.reshape(width, block), BATCH, spread)
    after, before = [down], []
    for s in range(1, nz // 2 + 1):
        after.append(shift(after[-1], "z", -1))
        if s < nz // 2:
            before.insert(0, shift(before[0] if before else down, "z", 1))
    down = turned(jnp.stack(after + before), (nz - z) % nz)

    by_chip = weight.reshape(ny, 2 * width, width)
    back_w = []
    for s in range(ny):
        piece = lax.dynamic_index_in_dim(by_chip, (y - s) % ny, 0, False)
        piece = (piece.astype(F32) * out_float[None, :]).astype(BF)
        back_w.append(shift(piece, "y", -s) if s else piece)

    ids_group = lax.dynamic_index_in_dim(ids_all.reshape(nx, nz, rows), z, 1, False)
    labels_group = lax.dynamic_index_in_dim(labels_all.reshape(nx, nz, rows), z, 1, False)
    owner = jnp.sum(
        jnp.where(
            ids_group[:, :, None] == jnp.arange(tower_owner.shape[0], dtype=jnp.int32),
            tower_owner[None, None, :],
            0,
        ),
        axis=2,
    )
    place = jnp.arange(rows, dtype=jnp.int32)
    rank = jnp.sum(
        (
            (ids_group[:, :, None] == ids_group[:, None, :])
            & (place[None, :, None] > place[None, None, :])
        ).astype(jnp.int32),
        axis=2,
    )
    slot = owner * (nx * cap) + jnp.arange(nx, dtype=jnp.int32)[:, None] * cap + rank
    placing = (
        jnp.arange(nb * nx * cap, dtype=jnp.int32)[:, None] == slot.reshape(1, group)
    ).astype(BF)

    pre = dot(feats, both_w, ((1,), (0,)))
    pre = turned(pre.reshape(nx, rows, 2 * block), (nx - x) % nx).reshape(group, 2 * block)
    gate_pre, up_pre = pre[:, :block], pre[:, block:]
    gate_sig = jax.nn.sigmoid(gate_pre)
    activated = gate_pre * gate_sig
    hidden_own = (activated * up_pre).astype(BF)
    hidden = jnp.concatenate(ring(hidden_own, "x"), axis=1)
    hidden, down, back_w = lax.optimization_barrier((hidden, down, back_w))
    halves = jnp.stack(back_w).reshape(ny, 2, width, width)
    back_own = lax.dynamic_index_in_dim(halves, c, 1, False)
    back_other = lax.dynamic_index_in_dim(halves, 1 - c, 1, False)
    back_other = lax.ppermute(back_other, "c", [(0, 1), (1, 0)])
    partial = jnp.einsum("rk,mkj->mrj", hidden, down, preferred_element_type=F32).astype(BF)
    trunk = jnp.sum(exchange(partial, MP).astype(F32), axis=0).astype(BF)

    outgoing = dot(placing, trunk, ((1,), (0,))).astype(BF)
    arrived = exchange(outgoing.reshape(nb, nx * cap, block), BATCH)
    tower_local = arrived.reshape(nx, slots, block).transpose(1, 0, 2).reshape(slots, width)
    tower, whose = [], []
    for s, piece in enumerate(ring(tower_local, "y")):
        tower += [piece, lax.ppermute(piece, "c", [(0, 1), (1, 0)])]
        whose += [(y + s) % ny * 2 + c, (y + s) % ny * 2 + 1 - c]

    whose = jnp.stack(whose).astype(jnp.int32)
    crossed, unscaled, logit_part = cross_layer(
        whose,
        tower,
        weight.reshape(nm, width, width),
        back_own,
        back_other,
        cross_b,
        out_w,
        nx,
    )
    local_float = tower_local.astype(F32)
    logit_part = logit_part.reshape(slots)

    part_by_z = logit_part.reshape(nz, nx * cap)
    high = part_by_z.astype(BF)
    low = (part_by_z - high.astype(F32)).astype(BF)
    tail = jnp.concatenate([high, low], axis=1)
    tail = jnp.concatenate([tail[:, None], jnp.zeros((nz, 7, block), BF)], axis=1)
    sent = unscaled.reshape(nx, nz, nx * cap, block)
    sent = jnp.concatenate([sent, jnp.broadcast_to(tail[None], (nx,) + tail.shape)], axis=2)
    returned = exchange(sent.reshape(nb, nx * cap + 8, block), BATCH)
    logit_sum = logit_part.reshape(nx, slots // nx)
    logit_sum = logit_sum + lax.ppermute(logit_sum, "c", [(0, 1), (1, 0)])
    for far in (1, 2):
        logit_sum = logit_sum + lax.ppermute(logit_sum, "y", [(i, i ^ far) for i in range(ny)])
    returned, logit_sum = lax.optimization_barrier((returned, logit_sum))
    row_cols = dot(placing, returned[:, : nx * cap].reshape(nb * nx * cap, block), ((0,), (0,)))
    logits = returned[:, nx * cap].reshape(nb, 2, nx * cap).transpose(1, 0, 2)
    logits = dot(logits.reshape(2, nb * nx * cap), placing, ((1,), (0,)))
    mixed = jnp.concatenate(
        [row_cols.astype(BF), logits.astype(BF).reshape(2 * nx, block)], axis=0
    )
    mixed = jnp.stack(ring(mixed, "y"))
    mixed = turned(jnp.stack(pair(mixed), axis=1), (ny - y) % ny)
    mixed = mixed.reshape(nm, group + 2 * nx, block)
    logit_rows = jnp.sum(mixed[:, group:].astype(F32), axis=0)
    logit_rows = logit_rows[:nx] + logit_rows[nx:]
    d_logit_rows = (jax.nn.sigmoid(logit_rows) - labels_group).reshape(group)
    by_row = d_logit_rows[:, None]
    d_rows = mixed[:, :group]

    d_hidden = jnp.einsum("mrj,mkj->rk", d_rows, down, preferred_element_type=F32)
    d_hidden = (d_hidden * by_row).astype(BF)
    d_parts = [d_hidden[:, s * block : (s + 1) * block] for s in range(nx)]
    d_hidden = d_parts[0].astype(F32)
    for s in range(1, nx):
        d_hidden = d_hidden + lax.ppermute(
            d_parts[s], "x", [(i, (i + s) % nx) for i in range(nx)]
        ).astype(F32)
    scaled_hidden = (hidden.astype(F32) * by_row).astype(BF)
    down_term = jnp.einsum("rk,mrj->mkj", scaled_hidden, d_rows, preferred_element_type=F32)
    down_term = down_term.astype(BF)
    term_for = lambda s: lax.dynamic_index_in_dim(down_term, (z + s) % nz, 0, False).astype(F32)
    total = term_for(0)
    for way, far in ((1, nz // 2), (-1, nz // 2 - 1)):
        moving = term_for(way * far)
        for s in range(1, far + 1):
            moving = shift(moving.astype(BF), "z", way).astype(F32)
            if s < far:
                moving = moving + term_for(way * (far - s))
        total = total + moving
    down_term = total.astype(BF)
    down_term = turned(down_term.reshape(nx, block, block), (nx - x) % nx).reshape(width, block)
    grad_down = lax.ppermute(down_term, BATCH, [(t, f) for f, t in spread]).astype(F32)
    d_up = d_hidden * activated
    d_gate = d_hidden * up_pre * gate_sig * (1.0 + gate_pre * (1.0 - gate_sig))
    d_both = jnp.concatenate([d_gate, d_up], axis=1).astype(BF).reshape(nx, rows, 2 * block)
    d_both = turned(d_both, x).reshape(group, 2 * block)
    term = dot(feats, d_both, ((0,), (0,))).astype(BF)
    term = exchange(term.reshape(nb, part, 2 * block), BATCH)
    term = jnp.sum(term.reshape(nx, nz, part, 2 * block).astype(F32), axis=1)
    flat = lambda t: t.transpose(1, 0, 2).reshape(part, nx * block)
    grad_gate, grad_up = flat(term[:, :, :block]), flat(term[:, :, block:])

    at = lax.axis_index(BATCH)
    mask = jnp.sum(
        jnp.where(
            ids_all[:, :, None] == jnp.arange(tower_owner.shape[0], dtype=jnp.int32),
            tower_owner[None, None, :],
            0,
        ),
        axis=2,
    ) == at
    before = jnp.sum(
        (mask[:, None, :] & (place[None, :, None] > place[None, None, :])).astype(jnp.int32), axis=2
    )
    slot_labels = jnp.sum(
        jnp.where(
            mask[:, :, None] & (before[:, :, None] == jnp.arange(cap, dtype=jnp.int32)),
            labels_all[:, :, None],
            0.0,
        ),
        axis=1,
    )
    slot_labels = slot_labels.reshape(nx, nz, cap).transpose(1, 0, 2).reshape(slots)
    d_logit = jax.nn.sigmoid(logit_sum.reshape(slots)) - slot_labels
    grad_outvec = jnp.sum(d_logit[:, None] * crossed, axis=0)
    d_pre = d_logit[:, None] * out_float[None, :] * local_float
    grad_bias = jnp.sum(d_pre, axis=0)
    d_pre_b = d_pre.astype(BF)
    grad_weight = cross_grad(whose, tower, d_pre_b).reshape(1, nm * width, width)
    return (grad_gate, grad_up, grad_down, grad_weight, grad_bias[None], grad_outvec[None])


def solution(mesh):
    split = Mesh(mesh.devices.reshape(4, 2, 4, 8), ("y", "c", "x", "z"))
    placed = (
        P(BATCH, None),
        P(BATCH),
        P(BATCH, None),
        P(),
        P(BATCH, MP),
        P(BATCH, MP),
        P(MP, BATCH),
        P(BATCH, None, MP),
        P(BATCH, MP),
        P(BATCH, MP),
    )
    return jax.shard_map(
        per_device,
        mesh=split,
        in_specs=placed,
        out_specs=(
            P(BATCH, MP),
            P(BATCH, MP),
            P(MP, BATCH),
            P(BATCH, None, MP),
            P(BATCH, MP),
            P(BATCH, MP),
        ),
        check_vma=False,
    )
```

```python
import jax
import jax.numpy as jnp
from jax import lax
from jax.experimental import pallas as pl
from jax.experimental.pallas import tpu as pltpu
from jax.sharding import Mesh, PartitionSpec as P

BATCH = ("x", "z")
MP = ("y", "c")
BF = jnp.bfloat16
F32 = jnp.float32


def ring(value, axis):
    count = lax.axis_size(axis)
    return [value] + [
        lax.ppermute(value, axis, [(i, (i - s) % count) for i in range(count)])
        for s in range(1, count)
    ]


def turned(stacked, start):
    count = stacked.shape[0]
    return lax.dynamic_slice_in_dim(jnp.concatenate([stacked, stacked]), start, count)


def exchange(value, axes):
    return lax.all_to_all(value, axes, split_axis=0, concat_axis=0, tiled=True)


def pair(value):
    other = lax.ppermute(value, "c", [(0, 1), (1, 0)])
    first = lax.axis_index("c") == 0
    return jnp.where(first, value, other), jnp.where(first, other, value)


def dot(left, right, contract):
    return lax.dot_general(left, right, (contract, ((), ())), preferred_element_type=F32)


def shift(value, axis, places):
    count = lax.axis_size(axis)
    return lax.ppermute(value, axis, [(i, (i + places) % count) for i in range(count)])


def cross_body(whose, *refs):
    pieces, others = refs[:-10], refs[-10:]
    rows_own, rows_other, back_own, back_other, bias, vector = others[:6]
    crossed, payload, pre_sum, back_sum = others[6:]
    steps = len(pieces) // 2
    step = pl.program_id(0)

    @pl.when(step == 0)
    def _():
        pre_sum[...] = jnp.zeros_like(pre_sum)
        back_sum[...] = jnp.zeros_like(back_sum)

    for k in range(steps):

        @pl.when(step == k)
        def _(k=k):
            piece = jnp.concatenate([pieces[2 * k][...], pieces[2 * k + 1][...]], axis=1)
            rows = jnp.concatenate([rows_own[0], rows_other[0]], axis=0)
            back = jnp.concatenate([back_own[0], back_other[0]], axis=1)
            pre_sum[...] += dot(piece, rows, ((1,), (0,)))
            back_sum[...] += dot(piece, back, ((1,), (1,)))

    @pl.when(step == steps - 1)
    def _():
        own = pieces[0][...].astype(F32)
        by = vector[...].astype(F32)
        shifted = pre_sum[...] + bias[...].astype(F32)
        whole = own * shifted + own
        slots, width = whole.shape
        crossed[...] = whole
        logit = jnp.sum(whole * by, axis=1, keepdims=True)
        across = jnp.transpose(jnp.broadcast_to(logit, (slots, 128)))[:16]
        high = across.astype(BF).astype(F32)
        line = lax.broadcasted_iota(jnp.int32, across.shape, 0)
        tail = jnp.where(line == 0, high, jnp.where(line == 1, across - high, 0.0)).astype(BF)
        result = (back_sum[...] + by * (shifted + 1.0)).astype(BF)
        parts, lines, lanes = payload.shape
        size = lines - 16
        places = slots // size
        for k in range(parts):
            i, j = k // places, k % places
            payload[k, 0:size, :] = result[j * size : (j + 1) * size, i * lanes : (i + 1) * lanes]
            at = j * size // lanes * lanes
            payload[k, size:lines, :] = tail[:, at : at + lanes]


def cross_layer(whose, pieces, weight, back_own, back_other, bias, vector, shape):
    count, slots, width = len(pieces), *pieces[0].shape
    whole = lambda shape: pl.BlockSpec(shape, lambda i, w: (0,) * len(shape))
    one = (1, width, width)
    half = pl.BlockSpec(one, lambda i, w: (i, 0, 0))
    rows_own = pl.BlockSpec(one, lambda i, w: (w[2 * i], 0, 0))
    rows_other = pl.BlockSpec(one, lambda i, w: (w[2 * i + 1], 0, 0))
    return pl.pallas_call(
        cross_body,
        grid_spec=pltpu.PrefetchScalarGridSpec(
            num_scalar_prefetch=1,
            grid=(count // 2,),
            in_specs=[whole((slots, width))] * count
            + [rows_own, rows_other, half, half]
            + [whole((1, width))] * 2,
            out_specs=[whole((slots, width)), whole(shape)],
            scratch_shapes=[pltpu.VMEM((slots, width), F32)] * 2,
        ),
        out_shape=[jax.ShapeDtypeStruct((slots, width), F32), jax.ShapeDtypeStruct(shape, BF)],
        compiler_params=pltpu.CompilerParams(vmem_limit_bytes=44 * 2**20),
        cost_estimate=pl.CostEstimate(
            flops=4 * count * slots * width * width,
            bytes_accessed=6 * count * width * width,
            transcendentals=0,
        ),
    )(whose, *pieces, weight, weight, back_own, back_other, bias, vector)


def grad_body(whose, *refs):
    pieces, right, out = refs[:-2], refs[-2], refs[-1]
    step = pl.program_id(0)
    for k in range(len(pieces)):

        @pl.when(step == k)
        def _(k=k):
            out[0] = dot(pieces[k][...], right[...], ((0,), (0,))).astype(BF)


def cross_grad(whose, pieces, right):
    count, slots, width = len(pieces), *pieces[0].shape
    return pl.pallas_call(
        grad_body,
        grid_spec=pltpu.PrefetchScalarGridSpec(
            num_scalar_prefetch=1,
            grid=(count,),
            in_specs=[pl.BlockSpec((slots, width), lambda i, w: (0, 0))] * (count + 1),
            out_specs=pl.BlockSpec((1, width, width), lambda i, w: (w[i], 0, 0)),
        ),
        out_shape=jax.ShapeDtypeStruct((count, width, width), BF),
        compiler_params=pltpu.CompilerParams(vmem_limit_bytes=44 * 2**20),
        cost_estimate=pl.CostEstimate(
            flops=2 * count * slots * width * width,
            bytes_accessed=4 * count * width * width,
            transcendentals=0,
        ),
    )(whose, *pieces, right)


def per_device(
    features, labels, scenario_ids, tower_owner, gate_w, up_w, down_w, cross_w, cross_b, out_w
):
    nx, nz, ny = lax.axis_size("x"), lax.axis_size("z"), lax.axis_size("y")
    nb, nm = nx * nz, 2 * ny
    x, z, y, c = (lax.axis_index(name) for name in ("x", "z", "y", "c"))
    rows, depth = features.shape
    part = gate_w.shape[0]
    width = cross_w.shape[2]
    block = down_w.shape[1]
    cap = 4 * rows // nb
    group = nx * rows
    slots = nb * cap
    weight = cross_w[0]
    out_float = out_w[0].astype(F32)

    blocks = ring(features, "x")
    aux = jnp.concatenate(
        [
            scenario_ids.reshape(1, rows).astype(BF),
            labels.reshape(1, rows),
            jnp.zeros((6, rows), BF),
        ],
        axis=0,
    )
    by_x = lambda w: w.reshape(part, nx, block).transpose(1, 0, 2)
    packed = jnp.concatenate(
        [by_x(gate_w), by_x(up_w), jnp.broadcast_to(aux[None], (nx, 8, rows))], axis=1
    )
    packed = jnp.broadcast_to(packed[:, None], (nx, nz) + packed.shape[1:])
    got = exchange(packed.reshape((nb,) + packed.shape[2:]), BATCH)
    both_w = jnp.concatenate([got[:, :part], got[:, part : 2 * part]], axis=2)
    both_w = both_w.reshape(depth, 2 * block)
    ids_all = got[:, 2 * part].astype(jnp.int32)
    labels_all = got[:, 2 * part + 1].astype(F32)

    spread = [(nx * m + i, i * nz + m) for m in range(nm) for i in range(nx)]
    turned_down = turned(down_w.reshape(nx, block, block), lax.axis_index(BATCH) % nx)
    down = lax.ppermute(turned_down.reshape(width, block), BATCH, spread)
    down, *blocks = lax.optimization_barrier((down, *blocks))
    down = exchange(jnp.broadcast_to(down[None], (nz, width, block)), "z")

    by_chip = weight.reshape(ny, 2 * width, width)
    back_w = []
    for s in range(ny):
        piece = lax.dynamic_index_in_dim(by_chip, (y - s) % ny, 0, False)
        piece = (piece.astype(F32) * out_float[None, :]).astype(BF)
        back_w.append(shift(piece, "y", -s) if s else piece)

    ids_group = lax.dynamic_index_in_dim(ids_all.reshape(nx, nz, rows), z, 1, False)
    labels_group = lax.dynamic_index_in_dim(labels_all.reshape(nx, nz, rows), z, 1, False)
    owner = jnp.sum(
        jnp.where(
            ids_group[:, :, None] == jnp.arange(tower_owner.shape[0], dtype=jnp.int32),
            tower_owner[None, None, :],
            0,
        ),
        axis=2,
    )
    place = jnp.arange(rows, dtype=jnp.int32)
    rank = jnp.sum(
        (
            (ids_group[:, :, None] == ids_group[:, None, :])
            & (place[None, :, None] > place[None, None, :])
        ).astype(jnp.int32),
        axis=2,
    )
    slot = owner * (nx * cap) + jnp.arange(nx, dtype=jnp.int32)[:, None] * cap + rank
    placing = (
        jnp.arange(nb * nx * cap, dtype=jnp.int32)[:, None] == slot.reshape(1, group)
    ).astype(BF)

    pre = jnp.stack([dot(part_rows, both_w, ((1,), (0,))) for part_rows in blocks])
    pre = turned(pre, (nx - x) % nx).reshape(group, 2 * block)
    gate_pre, up_pre = pre[:, :block], pre[:, block:]
    gate_sig = jax.nn.sigmoid(gate_pre)
    activated = gate_pre * gate_sig
    hidden_own = (activated * up_pre).astype(BF)
    hidden = jnp.concatenate(ring(hidden_own, "x"), axis=1)
    hidden, down, back_w = lax.optimization_barrier((hidden, down, back_w))
    halves = jnp.stack(back_w).reshape(ny, 2, width, width)
    back_own = lax.dynamic_index_in_dim(halves, c, 1, False)
    back_other = lax.dynamic_index_in_dim(halves, 1 - c, 1, False)
    back_other = lax.ppermute(back_other, "c", [(0, 1), (1, 0)])
    partial = jnp.einsum("rk,mkj->mrj", hidden, down, preferred_element_type=F32).astype(BF)
    trunk = jnp.sum(exchange(partial, MP).astype(F32), axis=0).astype(BF)

    trunk, *blocks = lax.optimization_barrier((trunk, *blocks))
    feats = jnp.concatenate(blocks, axis=0)

    outgoing = dot(placing, trunk, ((1,), (0,))).astype(BF)
    arrived = exchange(outgoing.reshape(nb, nx * cap, block), BATCH)
    tower_local = arrived.reshape(nx, slots, block).transpose(1, 0, 2).reshape(slots, width)
    tower, whose = [], []
    for s, piece in enumerate(ring(tower_local, "y")):
        tower += [piece, lax.ppermute(piece, "c", [(0, 1), (1, 0)])]
        whose += [(y + s) % ny * 2 + c, (y + s) % ny * 2 + 1 - c]

    whose = jnp.stack(whose).astype(jnp.int32)
    crossed, sent = cross_layer(
        whose,
        tower,
        weight.reshape(nm, width, width),
        back_own,
        back_other,
        cross_b,
        out_w,
        (nb, nx * cap + 16, block),
    )
    local_float = tower_local.astype(F32)

    returned = exchange(sent, BATCH)
    logit_part = jnp.sum(crossed * out_float[None, :], axis=1)
    logit_sum = logit_part.reshape(nx, slots // nx)
    logit_sum = logit_sum + lax.ppermute(logit_sum, "c", [(0, 1), (1, 0)])
    for far in (1, 2):
        logit_sum = logit_sum + lax.ppermute(logit_sum, "y", [(i, i ^ far) for i in range(ny)])

    at = lax.axis_index(BATCH)
    mask = jnp.sum(
        jnp.where(
            ids_all[:, :, None] == jnp.arange(tower_owner.shape[0], dtype=jnp.int32),
            tower_owner[None, None, :],
            0,
        ),
        axis=2,
    ) == at
    before = jnp.sum(
        (mask[:, None, :] & (place[None, :, None] > place[None, None, :])).astype(jnp.int32), axis=2
    )
    slot_labels = jnp.sum(
        jnp.where(
            mask[:, :, None] & (before[:, :, None] == jnp.arange(cap, dtype=jnp.int32)),
            labels_all[:, :, None],
            0.0,
        ),
        axis=1,
    )
    slot_labels = slot_labels.reshape(nx, nz, cap).transpose(1, 0, 2).reshape(slots)
    d_logit = jax.nn.sigmoid(logit_sum.reshape(slots)) - slot_labels
    grad_outvec = jnp.sum(d_logit[:, None] * crossed, axis=0)
    d_pre = d_logit[:, None] * out_float[None, :] * local_float
    grad_bias = jnp.sum(d_pre, axis=0)
    d_pre_b = d_pre.astype(BF)
    grad_weight = cross_grad(whose, tower, d_pre_b).reshape(1, nm * width, width)
    returned, grad_weight = lax.optimization_barrier((returned, grad_weight))

    row_cols = dot(placing, returned[:, : nx * cap].reshape(nb * nx * cap, block), ((0,), (0,)))
    per_row = block // (nx * cap)
    logits = returned[:, nx * cap : nx * cap + 2].reshape(nb, 2, per_row, nx * cap)
    logits = lax.dynamic_index_in_dim(logits, z % per_row, 2, False).transpose(1, 0, 2)
    logits = dot(logits.reshape(2, nb * nx * cap), placing, ((1,), (0,)))
    mixed = jnp.concatenate(
        [row_cols.astype(BF), logits.astype(BF).reshape(2 * nx, block)], axis=0
    )
    mixed = jnp.stack(ring(mixed, "y"))
    mixed = turned(jnp.stack(pair(mixed), axis=1), (ny - y) % ny)
    mixed = mixed.reshape(nm, group + 2 * nx, block)
    logit_rows = jnp.sum(mixed[:, group:].astype(F32), axis=0)
    logit_rows = logit_rows[:nx] + logit_rows[nx:]
    d_logit_rows = (jax.nn.sigmoid(logit_rows) - labels_group).reshape(group)
    by_row = d_logit_rows[:, None]
    d_rows = mixed[:, :group]

    d_hidden = jnp.einsum("mrj,mkj->rk", d_rows, down, preferred_element_type=F32)
    d_hidden = (d_hidden * by_row).astype(BF)
    d_parts = [d_hidden[:, s * block : (s + 1) * block] for s in range(nx)]
    d_hidden = d_parts[0].astype(F32)
    for s in range(1, nx):
        d_hidden = d_hidden + lax.ppermute(
            d_parts[s], "x", [(i, (i + s) % nx) for i in range(nx)]
        ).astype(F32)
    scaled_hidden = (hidden.astype(F32) * by_row).astype(BF)
    down_term = jnp.einsum("rk,mrj->mkj", scaled_hidden, d_rows, preferred_element_type=F32)
    d_up = d_hidden * activated
    d_gate = d_hidden * up_pre * gate_sig * (1.0 + gate_pre * (1.0 - gate_sig))
    d_both = jnp.concatenate([d_gate, d_up], axis=1).astype(BF).reshape(nx, rows, 2 * block)
    d_both = turned(d_both, x).reshape(group, 2 * block)
    term = dot(feats, d_both, ((0,), (0,))).astype(BF)
    down_term = down_term.astype(BF)
    term_for = lambda s: lax.dynamic_index_in_dim(down_term, (z + s) % nz, 0, False)
    far = nz // 2 - 1
    total = term_for(0).astype(F32) + shift(term_for(far + 1), "z", far + 1).astype(F32)
    forth, back = term_for(far), term_for(-far)
    for s in range(1, far + 1):
        forth, back = shift(forth, "z", 1), shift(back, "z", -1)
        if s < far:
            forth = (forth.astype(F32) + term_for(far - s).astype(F32)).astype(BF)
            back = (back.astype(F32) + term_for(s - far).astype(F32)).astype(BF)
        if s == far - 1:
            forth, back, term = lax.optimization_barrier((forth, back, term))
    down_term = (total + forth.astype(F32) + back.astype(F32)).astype(BF)
    down_term = turned(down_term.reshape(nx, block, block), (nx - x) % nx).reshape(width, block)
    grad_down = lax.ppermute(down_term, BATCH, [(t, f) for f, t in spread]).astype(F32)
    term = exchange(term.reshape(nb, part, 2 * block), BATCH)
    term = jnp.sum(term.reshape(nx, nz, part, 2 * block).astype(F32), axis=1)
    flat = lambda t: t.transpose(1, 0, 2).reshape(part, nx * block)
    grad_gate, grad_up = flat(term[:, :, :block]), flat(term[:, :, block:])

    return (grad_gate, grad_up, grad_down, grad_weight, grad_bias[None], grad_outvec[None])


def solution(mesh):
    split = Mesh(mesh.devices.reshape(4, 2, 4, 8), ("y", "c", "x", "z"))
    placed = (
        P(BATCH, None),
        P(BATCH),
        P(BATCH, None),
        P(),
        P(BATCH, MP),
        P(BATCH, MP),
        P(MP, BATCH),
        P(BATCH, None, MP),
        P(BATCH, MP),
        P(BATCH, MP),
    )
    return jax.shard_map(
        per_device,
        mesh=split,
        in_specs=placed,
        out_specs=(
            P(BATCH, MP),
            P(BATCH, MP),
            P(MP, BATCH),
            P(BATCH, None, MP),
            P(BATCH, MP),
            P(BATCH, MP),
        ),
        check_vma=False,
    )
```

```python
import jax
import jax.numpy as jnp
from jax import lax
from jax.experimental import pallas as pl
from jax.experimental.pallas import tpu as pltpu
from jax.sharding import Mesh, PartitionSpec as P

BATCH = ("x", "z")
MP = ("y", "c")
BF = jnp.bfloat16
F32 = jnp.float32


def ring(value, axis):
    count = lax.axis_size(axis)
    return [value] + [
        lax.ppermute(value, axis, [(i, (i - s) % count) for i in range(count)])
        for s in range(1, count)
    ]


def turned(stacked, start):
    count = stacked.shape[0]
    return lax.dynamic_slice_in_dim(jnp.concatenate([stacked, stacked]), start, count)


def exchange(value, axes):
    return lax.all_to_all(value, axes, split_axis=0, concat_axis=0, tiled=True)


def pair(value):
    other = lax.ppermute(value, "c", [(0, 1), (1, 0)])
    first = lax.axis_index("c") == 0
    return jnp.where(first, value, other), jnp.where(first, other, value)


def dot(left, right, contract):
    return lax.dot_general(left, right, (contract, ((), ())), preferred_element_type=F32)


def shift(value, axis, places):
    count = lax.axis_size(axis)
    return lax.ppermute(value, axis, [(i, (i + places) % count) for i in range(count)])


def cross_body(whose, *refs):
    pieces, others = refs[:-10], refs[-10:]
    rows_own, rows_other, back_own, back_other, bias, vector = others[:6]
    crossed, payload, pre_sum, back_sum = others[6:]
    steps = len(pieces) // 2
    step = pl.program_id(0)

    @pl.when(step == 0)
    def _():
        pre_sum[...] = jnp.zeros_like(pre_sum)
        back_sum[...] = jnp.zeros_like(back_sum)

    for k in range(steps):

        @pl.when(step == k)
        def _(k=k):
            piece = jnp.concatenate([pieces[2 * k][...], pieces[2 * k + 1][...]], axis=1)
            rows = jnp.concatenate([rows_own[0], rows_other[0]], axis=0)
            back = jnp.concatenate([back_own[0], back_other[0]], axis=1)
            pre_sum[...] += dot(piece, rows, ((1,), (0,)))
            back_sum[...] += dot(piece, back, ((1,), (1,)))

    @pl.when(step == steps - 1)
    def _():
        own = pieces[0][...].astype(F32)
        by = vector[...].astype(F32)
        shifted = pre_sum[...] + bias[...].astype(F32)
        whole = own * shifted + own
        slots, width = whole.shape
        crossed[...] = whole
        logit = jnp.sum(whole * by, axis=1, keepdims=True)
        across = jnp.transpose(jnp.broadcast_to(logit, (slots, 128)))[:16]
        high = across.astype(BF).astype(F32)
        line = lax.broadcasted_iota(jnp.int32, across.shape, 0)
        tail = jnp.where(line == 0, high, jnp.where(line == 1, across - high, 0.0)).astype(BF)
        result = (back_sum[...] + by * (shifted + 1.0)).astype(BF)
        parts, lines, lanes = payload.shape
        size = lines - 16
        places = slots // size
        for k in range(parts):
            i, j = k // places, k % places
            payload[k, 0:size, :] = result[j * size : (j + 1) * size, i * lanes : (i + 1) * lanes]
            at = j * size // lanes * lanes
            payload[k, size:lines, :] = tail[:, at : at + lanes]


def cross_layer(whose, pieces, weight, back_own, back_other, bias, vector, shape):
    count, slots, width = len(pieces), *pieces[0].shape
    whole = lambda shape: pl.BlockSpec(shape, lambda i, w: (0,) * len(shape))
    one = (1, width, width)
    half = pl.BlockSpec(one, lambda i, w: (i, 0, 0))
    rows_own = pl.BlockSpec(one, lambda i, w: (w[2 * i], 0, 0))
    rows_other = pl.BlockSpec(one, lambda i, w: (w[2 * i + 1], 0, 0))
    return pl.pallas_call(
        cross_body,
        grid_spec=pltpu.PrefetchScalarGridSpec(
            num_scalar_prefetch=1,
            grid=(count // 2,),
            in_specs=[whole((slots, width))] * count
            + [rows_own, rows_other, half, half]
            + [whole((1, width))] * 2,
            out_specs=[whole((slots, width)), whole(shape)],
            scratch_shapes=[pltpu.VMEM((slots, width), F32)] * 2,
        ),
        out_shape=[jax.ShapeDtypeStruct((slots, width), F32), jax.ShapeDtypeStruct(shape, BF)],
        compiler_params=pltpu.CompilerParams(vmem_limit_bytes=44 * 2**20),
        cost_estimate=pl.CostEstimate(
            flops=4 * count * slots * width * width,
            bytes_accessed=6 * count * width * width,
            transcendentals=0,
        ),
    )(whose, *pieces, weight, weight, back_own, back_other, bias, vector)


def grad_body(whose, *refs):
    pieces, right, out = refs[:-2], refs[-2], refs[-1]
    step = pl.program_id(0)
    for k in range(len(pieces)):

        @pl.when(step == k)
        def _(k=k):
            out[0] = dot(pieces[k][...], right[...], ((0,), (0,))).astype(BF)


def cross_grad(whose, pieces, right):
    count, slots, width = len(pieces), *pieces[0].shape
    return pl.pallas_call(
        grad_body,
        grid_spec=pltpu.PrefetchScalarGridSpec(
            num_scalar_prefetch=1,
            grid=(count,),
            in_specs=[pl.BlockSpec((slots, width), lambda i, w: (0, 0))] * (count + 1),
            out_specs=pl.BlockSpec((1, width, width), lambda i, w: (w[i], 0, 0)),
        ),
        out_shape=jax.ShapeDtypeStruct((count, width, width), BF),
        compiler_params=pltpu.CompilerParams(vmem_limit_bytes=44 * 2**20),
        cost_estimate=pl.CostEstimate(
            flops=2 * count * slots * width * width,
            bytes_accessed=4 * count * width * width,
            transcendentals=0,
        ),
    )(whose, *pieces, right)


def per_device(
    features, labels, scenario_ids, tower_owner, gate_w, up_w, down_w, cross_w, cross_b, out_w
):
    nx, nz, ny = lax.axis_size("x"), lax.axis_size("z"), lax.axis_size("y")
    nb, nm = nx * nz, 2 * ny
    x, z, y, c = (lax.axis_index(name) for name in ("x", "z", "y", "c"))
    rows, depth = features.shape
    part = gate_w.shape[0]
    width = cross_w.shape[2]
    block = down_w.shape[1]
    cap = 4 * rows // nb
    group = nx * rows
    slots = nb * cap
    weight = cross_w[0]
    out_float = out_w[0].astype(F32)

    spread = [(nx * m + i, i * nz + m) for m in range(nm) for i in range(nx)]
    turned_down = turned(down_w.reshape(nx, block, block), lax.axis_index(BATCH) % nx)
    down = lax.ppermute(turned_down.reshape(width, block), BATCH, spread)

    half_depth = depth // 2
    half_of = lambda v, core, axis: lax.dynamic_slice_in_dim(v, core * half_depth, half_depth, axis)
    mine = [half_of(features, c, 1)]
    for s in range(1, nx - 1):
        mine.append(shift(mine[-1], "x", -1))
    mine.append(shift(mine[0], "x", 1))
    down, *mine = lax.optimization_barrier((down, *mine))
    theirs = lax.ppermute(jnp.concatenate(mine[1:], axis=0), "c", [(0, 1), (1, 0)])
    mine = jnp.concatenate(mine, axis=0)
    theirs = jnp.concatenate([half_of(features, 1 - c, 1), theirs], axis=0)
    aux = jnp.concatenate(
        [
            scenario_ids.reshape(1, rows).astype(BF),
            labels.reshape(1, rows),
            jnp.zeros((6, rows), BF),
        ],
        axis=0,
    )
    by_x = lambda w: w.reshape(part, nx, block).transpose(1, 0, 2)
    packed = jnp.concatenate(
        [by_x(gate_w), by_x(up_w), jnp.broadcast_to(aux[None], (nx, 8, rows))], axis=1
    )
    packed = jnp.broadcast_to(packed[:, None], (nx, nz) + packed.shape[1:])
    got = exchange(packed.reshape((nb,) + packed.shape[2:]), BATCH)
    both_w = jnp.concatenate([got[:, :part], got[:, part : 2 * part]], axis=2)
    both_w = both_w.reshape(depth, 2 * block)
    ids_all = got[:, 2 * part].astype(jnp.int32)
    labels_all = got[:, 2 * part + 1].astype(F32)

    by_chip = weight.reshape(ny, 2 * width, width)
    back_w = []
    for s in range(ny):
        piece = lax.dynamic_index_in_dim(by_chip, (y - s) % ny, 0, False)
        piece = (piece.astype(F32) * out_float[None, :]).astype(BF)
        if s in (1, ny - 1):
            piece = shift(piece, "y", -s)
        back_w.append(piece)

    down, mine, theirs, back_w = lax.optimization_barrier((down, mine, theirs, back_w))
    back_w = [
        piece if s in (0, 1, ny - 1) else shift(piece, "y", -s) for s, piece in enumerate(back_w)
    ]
    down = exchange(jnp.broadcast_to(down[None], (nz, width, block)), "z")

    ids_group = lax.dynamic_index_in_dim(ids_all.reshape(nx, nz, rows), z, 1, False)
    labels_group = lax.dynamic_index_in_dim(labels_all.reshape(nx, nz, rows), z, 1, False)
    owner = jnp.sum(
        jnp.where(
            ids_group[:, :, None] == jnp.arange(tower_owner.shape[0], dtype=jnp.int32),
            tower_owner[None, None, :],
            0,
        ),
        axis=2,
    )
    place = jnp.arange(rows, dtype=jnp.int32)
    rank = jnp.sum(
        (
            (ids_group[:, :, None] == ids_group[:, None, :])
            & (place[None, :, None] > place[None, None, :])
        ).astype(jnp.int32),
        axis=2,
    )
    slot = owner * (nx * cap) + jnp.arange(nx, dtype=jnp.int32)[:, None] * cap + rank
    stride = nx * cap + 16
    placing_back = (
        jnp.arange(nb * stride, dtype=jnp.int32)[:, None]
        == (slot + owner * (stride - nx * cap)).reshape(1, group)
    ).astype(BF)
    placing = (
        jnp.arange(nb * nx * cap, dtype=jnp.int32)[:, None] == slot.reshape(1, group)
    ).astype(BF)

    pre = dot(mine, half_of(both_w, c, 0), ((1,), (0,)))
    pre = pre + dot(theirs, half_of(both_w, 1 - c, 0), ((1,), (0,)))
    pre = pre.reshape(nx, rows, 2 * block)
    pre = turned(pre, (nx - x) % nx).reshape(group, 2 * block)
    gate_pre, up_pre = pre[:, :block], pre[:, block:]
    gate_sig = jax.nn.sigmoid(gate_pre)
    activated = gate_pre * gate_sig
    hidden_own = (activated * up_pre).astype(BF)
    hidden = jnp.concatenate(ring(hidden_own, "x"), axis=1)
    hidden, down, back_w = lax.optimization_barrier((hidden, down, back_w))
    halves = jnp.stack(back_w).reshape(ny, 2, width, width)
    back_own = lax.dynamic_index_in_dim(halves, c, 1, False)
    back_other = lax.dynamic_index_in_dim(halves, 1 - c, 1, False)
    back_other = lax.ppermute(back_other, "c", [(0, 1), (1, 0)])
    partial = jnp.einsum("rk,mkj->mrj", hidden, down, preferred_element_type=F32).astype(BF)
    trunk = jnp.sum(exchange(partial, MP).astype(F32), axis=0).astype(BF)

    trunk, mine, theirs = lax.optimization_barrier((trunk, mine, theirs))
    feats = jnp.concatenate(
        [jnp.where(c == 0, mine, theirs), jnp.where(c == 0, theirs, mine)], axis=1
    )

    outgoing = dot(placing, trunk, ((1,), (0,))).astype(BF)
    arrived = exchange(outgoing.reshape(nb, nx * cap, block), BATCH)
    tower_local = arrived.reshape(nx, slots, block).transpose(1, 0, 2).reshape(slots, width)
    tower, whose = [], []
    for s, piece in enumerate(ring(tower_local, "y")):
        tower += [piece, lax.ppermute(piece, "c", [(0, 1), (1, 0)])]
        whose += [(y + s) % ny * 2 + c, (y + s) % ny * 2 + 1 - c]

    whose = jnp.stack(whose).astype(jnp.int32)
    crossed, sent = cross_layer(
        whose,
        tower,
        weight.reshape(nm, width, width),
        back_own,
        back_other,
        cross_b,
        out_w,
        (nb, nx * cap + 16, block),
    )
    local_float = tower_local.astype(F32)

    returned = exchange(sent, BATCH)
    logit_part = jnp.sum(crossed * out_float[None, :], axis=1)
    logit_sum = logit_part.reshape(nx, slots // nx)
    logit_sum = logit_sum + lax.ppermute(logit_sum, "c", [(0, 1), (1, 0)])
    for far in (1, 2):
        logit_sum = logit_sum + lax.ppermute(logit_sum, "y", [(i, i ^ far) for i in range(ny)])

    at = lax.axis_index(BATCH)
    mask = jnp.sum(
        jnp.where(
            ids_all[:, :, None] == jnp.arange(tower_owner.shape[0], dtype=jnp.int32),
            tower_owner[None, None, :],
            0,
        ),
        axis=2,
    ) == at
    before = jnp.sum(
        (mask[:, None, :] & (place[None, :, None] > place[None, None, :])).astype(jnp.int32), axis=2
    )
    slot_labels = jnp.sum(
        jnp.where(
            mask[:, :, None] & (before[:, :, None] == jnp.arange(cap, dtype=jnp.int32)),
            labels_all[:, :, None],
            0.0,
        ),
        axis=1,
    )
    slot_labels = slot_labels.reshape(nx, nz, cap).transpose(1, 0, 2).reshape(slots)
    d_logit = jax.nn.sigmoid(logit_sum.reshape(slots)) - slot_labels
    grad_outvec = jnp.sum(d_logit[:, None] * crossed, axis=0)
    d_pre = d_logit[:, None] * out_float[None, :] * local_float
    grad_bias = jnp.sum(d_pre, axis=0)
    d_pre_b = d_pre.astype(BF)
    grad_weight = cross_grad(whose, tower, d_pre_b).reshape(1, nm * width, width)
    returned, grad_weight = lax.optimization_barrier((returned, grad_weight))

    row_cols = dot(placing_back, returned.reshape(nb * stride, block), ((0,), (0,)))
    per_row = block // (nx * cap)
    logits = returned[:, nx * cap : nx * cap + 2].reshape(nb, 2, per_row, nx * cap)
    logits = lax.dynamic_index_in_dim(logits, z % per_row, 2, False).transpose(1, 0, 2)
    logits = dot(logits.reshape(2, nb * nx * cap), placing, ((1,), (0,)))
    mixed = jnp.concatenate(
        [row_cols.astype(BF), logits.astype(BF).reshape(2 * nx, block)], axis=0
    )
    mixed = jnp.stack(ring(mixed, "y"))
    mixed = turned(jnp.stack(pair(mixed), axis=1), (ny - y) % ny)
    mixed = mixed.reshape(nm, group + 2 * nx, block)
    logit_rows = jnp.sum(mixed[:, group:].astype(F32), axis=0)
    logit_rows = logit_rows[:nx] + logit_rows[nx:]
    d_logit_rows = (jax.nn.sigmoid(logit_rows) - labels_group).reshape(group)
    by_row = d_logit_rows[:, None]
    d_rows = mixed[:, :group]

    d_hidden = jnp.einsum("mrj,mkj->rk", d_rows, down, preferred_element_type=F32)
    d_hidden = (d_hidden * by_row).astype(BF)
    d_parts = [d_hidden[:, s * block : (s + 1) * block] for s in range(nx)]
    d_hidden = d_parts[0].astype(F32)
    for s in range(1, nx):
        d_hidden = d_hidden + lax.ppermute(
            d_parts[s], "x", [(i, (i + s) % nx) for i in range(nx)]
        ).astype(F32)
    scaled_hidden = (hidden.astype(F32) * by_row).astype(BF)
    down_term = jnp.einsum("rk,mrj->mkj", scaled_hidden, d_rows, preferred_element_type=F32)
    d_up = d_hidden * activated
    d_gate = d_hidden * up_pre * gate_sig * (1.0 + gate_pre * (1.0 - gate_sig))
    d_both = jnp.concatenate([d_gate, d_up], axis=1).astype(BF).reshape(nx, rows, 2 * block)
    d_both = turned(d_both, x).reshape(group, 2 * block)
    term = dot(feats, d_both, ((0,), (0,))).astype(BF)
    down_term = down_term.astype(BF)
    term_for = lambda s: lax.dynamic_index_in_dim(down_term, (z + s) % nz, 0, False)
    far = nz // 2 - 1
    total = term_for(0).astype(F32) + shift(term_for(far + 1), "z", far + 1).astype(F32)
    forth, back = term_for(far), term_for(-far)
    for s in range(1, far + 1):
        forth, back = shift(forth, "z", 1), shift(back, "z", -1)
        if s < far:
            forth = (forth.astype(F32) + term_for(far - s).astype(F32)).astype(BF)
            back = (back.astype(F32) + term_for(s - far).astype(F32)).astype(BF)
        if s == far - 1:
            forth, back, term = lax.optimization_barrier((forth, back, term))
    down_term = (total + forth.astype(F32) + back.astype(F32)).astype(BF)
    down_term = turned(down_term.reshape(nx, block, block), (nx - x) % nx).reshape(width, block)
    grad_down = lax.ppermute(down_term, BATCH, [(t, f) for f, t in spread]).astype(F32)
    term = exchange(term.reshape(nb, part, 2 * block), BATCH)
    term = jnp.sum(term.reshape(nx, nz, part, 2 * block).astype(F32), axis=1)
    flat = lambda t: t.transpose(1, 0, 2).reshape(part, nx * block)
    grad_gate, grad_up = flat(term[:, :, :block]), flat(term[:, :, block:])

    return (grad_gate, grad_up, grad_down, grad_weight, grad_bias[None], grad_outvec[None])


def solution(mesh):
    split = Mesh(mesh.devices.reshape(4, 2, 4, 8), ("y", "c", "x", "z"))
    placed = (
        P(BATCH, None),
        P(BATCH),
        P(BATCH, None),
        P(),
        P(BATCH, MP),
        P(BATCH, MP),
        P(MP, BATCH),
        P(BATCH, None, MP),
        P(BATCH, MP),
        P(BATCH, MP),
    )
    return jax.shard_map(
        per_device,
        mesh=split,
        in_specs=placed,
        out_specs=(
            P(BATCH, MP),
            P(BATCH, MP),
            P(MP, BATCH),
            P(BATCH, None, MP),
            P(BATCH, MP),
            P(BATCH, MP),
        ),
        check_vma=False,
    )
```

```python
import jax
import jax.numpy as jnp
from jax import lax
from jax.experimental import pallas as pl
from jax.experimental.pallas import tpu as pltpu
from jax.sharding import Mesh, PartitionSpec as P

BATCH = ("x", "z")
MP = ("y", "c")
BF = jnp.bfloat16
F32 = jnp.float32


def ring(value, axis):
    count = lax.axis_size(axis)
    return [value] + [
        lax.ppermute(value, axis, [(i, (i - s) % count) for i in range(count)])
        for s in range(1, count)
    ]


def turned(stacked, start):
    count = stacked.shape[0]
    return lax.dynamic_slice_in_dim(jnp.concatenate([stacked, stacked]), start, count)


def exchange(value, axes):
    return lax.all_to_all(value, axes, split_axis=0, concat_axis=0, tiled=True)


def pair(value):
    other = lax.ppermute(value, "c", [(0, 1), (1, 0)])
    first = lax.axis_index("c") == 0
    return jnp.where(first, value, other), jnp.where(first, other, value)


def dot(left, right, contract):
    return lax.dot_general(left, right, (contract, ((), ())), preferred_element_type=F32)


def shift(value, axis, places):
    count = lax.axis_size(axis)
    return lax.ppermute(value, axis, [(i, (i + places) % count) for i in range(count)])


def cross_body(whose, *refs):
    pieces, others = refs[:-10], refs[-10:]
    rows_own, rows_other, back_own, back_other, bias, vector = others[:6]
    crossed, payload, pre_sum, back_sum = others[6:]
    steps = len(pieces) // 2
    step = pl.program_id(0)

    @pl.when(step == 0)
    def _():
        pre_sum[...] = jnp.zeros_like(pre_sum)
        back_sum[...] = jnp.zeros_like(back_sum)

    for k in range(steps):

        @pl.when(step == k)
        def _(k=k):
            piece = jnp.concatenate([pieces[2 * k][...], pieces[2 * k + 1][...]], axis=1)
            rows = jnp.concatenate([rows_own[0], rows_other[0]], axis=0)
            back = jnp.concatenate([back_own[0], back_other[0]], axis=1)
            pre_sum[...] += dot(piece, rows, ((1,), (0,)))
            back_sum[...] += dot(piece, back, ((1,), (1,)))

    @pl.when(step == steps - 1)
    def _():
        own = pieces[0][...].astype(F32)
        by = vector[...].astype(F32)
        shifted = pre_sum[...] + bias[...].astype(F32)
        whole = own * shifted + own
        slots, width = whole.shape
        crossed[...] = whole
        logit = jnp.sum(whole * by, axis=1, keepdims=True)
        across = jnp.transpose(jnp.broadcast_to(logit, (slots, 128)))[:16]
        high = across.astype(BF).astype(F32)
        line = lax.broadcasted_iota(jnp.int32, across.shape, 0)
        tail = jnp.where(line == 0, high, jnp.where(line == 1, across - high, 0.0)).astype(BF)
        result = (back_sum[...] + by * (shifted + 1.0)).astype(BF)
        parts, lines, lanes = payload.shape
        size = lines - 16
        places = slots // size
        for k in range(parts):
            i, j = k // places, k % places
            payload[k, 0:size, :] = result[j * size : (j + 1) * size, i * lanes : (i + 1) * lanes]
            at = j * size // lanes * lanes
            payload[k, size:lines, :] = tail[:, at : at + lanes]


def cross_layer(whose, pieces, weight, back_own, back_other, bias, vector, shape):
    count, slots, width = len(pieces), *pieces[0].shape
    whole = lambda shape: pl.BlockSpec(shape, lambda i, w: (0,) * len(shape))
    one = (1, width, width)
    half = pl.BlockSpec(one, lambda i, w: (i, 0, 0))
    rows_own = pl.BlockSpec(one, lambda i, w: (w[2 * i], 0, 0))
    rows_other = pl.BlockSpec(one, lambda i, w: (w[2 * i + 1], 0, 0))
    return pl.pallas_call(
        cross_body,
        grid_spec=pltpu.PrefetchScalarGridSpec(
            num_scalar_prefetch=1,
            grid=(count // 2,),
            in_specs=[whole((slots, width))] * count
            + [rows_own, rows_other, half, half]
            + [whole((1, width))] * 2,
            out_specs=[whole((slots, width)), whole(shape)],
            scratch_shapes=[pltpu.VMEM((slots, width), F32)] * 2,
        ),
        out_shape=[jax.ShapeDtypeStruct((slots, width), F32), jax.ShapeDtypeStruct(shape, BF)],
        compiler_params=pltpu.CompilerParams(vmem_limit_bytes=44 * 2**20),
        cost_estimate=pl.CostEstimate(
            flops=4 * count * slots * width * width,
            bytes_accessed=6 * count * width * width,
            transcendentals=0,
        ),
    )(whose, *pieces, weight, weight, back_own, back_other, bias, vector)


def grad_body(whose, *refs):
    pieces, right, out = refs[:-2], refs[-2], refs[-1]
    step = pl.program_id(0)
    for k in range(len(pieces)):

        @pl.when(step == k)
        def _(k=k):
            out[0] = dot(pieces[k][...], right[...], ((0,), (0,))).astype(BF)


def cross_grad(whose, pieces, right):
    count, slots, width = len(pieces), *pieces[0].shape
    return pl.pallas_call(
        grad_body,
        grid_spec=pltpu.PrefetchScalarGridSpec(
            num_scalar_prefetch=1,
            grid=(count,),
            in_specs=[pl.BlockSpec((slots, width), lambda i, w: (0, 0))] * (count + 1),
            out_specs=pl.BlockSpec((1, width, width), lambda i, w: (w[i], 0, 0)),
        ),
        out_shape=jax.ShapeDtypeStruct((count, width, width), BF),
        compiler_params=pltpu.CompilerParams(vmem_limit_bytes=44 * 2**20),
        cost_estimate=pl.CostEstimate(
            flops=2 * count * slots * width * width,
            bytes_accessed=4 * count * width * width,
            transcendentals=0,
        ),
    )(whose, *pieces, right)


def per_device(
    features, labels, scenario_ids, tower_owner, gate_w, up_w, down_w, cross_w, cross_b, out_w
):
    nx, nz, ny = lax.axis_size("x"), lax.axis_size("z"), lax.axis_size("y")
    nb, nm = nx * nz, 2 * ny
    x, z, y, c = (lax.axis_index(name) for name in ("x", "z", "y", "c"))
    rows, depth = features.shape
    part = gate_w.shape[0]
    width = cross_w.shape[2]
    block = down_w.shape[1]
    cap = 4 * rows // nb
    group = nx * rows
    slots = nb * cap
    weight = cross_w[0]
    out_float = out_w[0].astype(F32)

    spread = [(nx * m + i, i * nz + m) for m in range(nm) for i in range(nx)]
    turned_down = turned(down_w.reshape(nx, block, block), lax.axis_index(BATCH) % nx)
    down = lax.ppermute(turned_down.reshape(width, block), BATCH, spread)

    half_depth = depth // 2
    half_of = lambda v, core, axis: lax.dynamic_slice_in_dim(v, core * half_depth, half_depth, axis)
    mine = [half_of(features, c, 1)]
    for s in range(1, nx - 1):
        mine.append(shift(mine[-1], "x", -1))
    mine.append(shift(mine[0], "x", 1))
    down, *mine = lax.optimization_barrier((down, *mine))
    theirs = lax.ppermute(jnp.concatenate(mine[1:], axis=0), "c", [(0, 1), (1, 0)])
    mine = jnp.concatenate(mine, axis=0)
    theirs = jnp.concatenate([half_of(features, 1 - c, 1), theirs], axis=0)
    aux = jnp.concatenate(
        [
            scenario_ids.reshape(1, rows).astype(BF),
            labels.reshape(1, rows),
            jnp.zeros((6, rows), BF),
        ],
        axis=0,
    )
    by_x = lambda w: w.reshape(part, nx, block).transpose(1, 0, 2)
    packed = jnp.concatenate(
        [by_x(gate_w), by_x(up_w), jnp.broadcast_to(aux[None], (nx, 8, rows))], axis=1
    )
    packed = jnp.broadcast_to(packed[:, None], (nx, nz) + packed.shape[1:])
    got = exchange(packed.reshape((nb,) + packed.shape[2:]), BATCH)
    both_w = jnp.concatenate([got[:, :part], got[:, part : 2 * part]], axis=2)
    both_w = both_w.reshape(depth, 2 * block)
    ids_all = got[:, 2 * part].astype(jnp.int32)
    labels_all = got[:, 2 * part + 1].astype(F32)

    by_chip = weight.reshape(ny, 2 * width, width)
    back_w = []
    for s in range(ny):
        piece = lax.dynamic_index_in_dim(by_chip, (y - s) % ny, 0, False)
        piece = (piece.astype(F32) * out_float[None, :]).astype(BF)
        if s in (1, ny - 1):
            piece = shift(piece, "y", -s)
        back_w.append(piece)

    down, mine, theirs, back_w = lax.optimization_barrier((down, mine, theirs, back_w))
    back_w = [
        piece if s in (0, 1, ny - 1) else shift(piece, "y", -s) for s, piece in enumerate(back_w)
    ]
    down = exchange(jnp.broadcast_to(down[None], (nz, width, block)), "z")

    ids_group = lax.dynamic_index_in_dim(ids_all.reshape(nx, nz, rows), z, 1, False)
    labels_group = lax.dynamic_index_in_dim(labels_all.reshape(nx, nz, rows), z, 1, False)
    owner = jnp.sum(
        jnp.where(
            ids_group[:, :, None] == jnp.arange(tower_owner.shape[0], dtype=jnp.int32),
            tower_owner[None, None, :],
            0,
        ),
        axis=2,
    )
    place = jnp.arange(rows, dtype=jnp.int32)
    rank = jnp.sum(
        (
            (ids_group[:, :, None] == ids_group[:, None, :])
            & (place[None, :, None] > place[None, None, :])
        ).astype(jnp.int32),
        axis=2,
    )
    slot = owner * (nx * cap) + jnp.arange(nx, dtype=jnp.int32)[:, None] * cap + rank
    stride = nx * cap + 16
    placing_back = (
        jnp.arange(nb * stride, dtype=jnp.int32)[:, None]
        == (slot + owner * (stride - nx * cap)).reshape(1, group)
    ).astype(BF)
    placing = (
        jnp.arange(nb * nx * cap, dtype=jnp.int32)[:, None] == slot.reshape(1, group)
    ).astype(BF)

    pre = dot(mine, half_of(both_w, c, 0), ((1,), (0,)))
    pre = pre + dot(theirs, half_of(both_w, 1 - c, 0), ((1,), (0,)))
    pre = pre.reshape(nx, rows, 2 * block)
    pre = turned(pre, (nx - x) % nx).reshape(group, 2 * block)
    gate_pre, up_pre = pre[:, :block], pre[:, block:]
    gate_sig = jax.nn.sigmoid(gate_pre)
    activated = gate_pre * gate_sig
    hidden_own = (activated * up_pre).astype(BF)
    hidden = jnp.concatenate(ring(hidden_own, "x"), axis=1)
    hidden, down, back_w = lax.optimization_barrier((hidden, down, back_w))
    halves = jnp.stack(back_w).reshape(ny, 2, width, width)
    back_own = lax.dynamic_index_in_dim(halves, c, 1, False)
    back_other = lax.dynamic_index_in_dim(halves, 1 - c, 1, False)
    back_other = lax.ppermute(back_other, "c", [(0, 1), (1, 0)])
    partial = jnp.einsum("rk,mkj->mrj", hidden, down, preferred_element_type=F32).astype(BF)
    trunk = jnp.sum(exchange(partial, MP).astype(F32), axis=0).astype(BF)

    trunk, mine, theirs = lax.optimization_barrier((trunk, mine, theirs))
    feats = jnp.concatenate(
        [jnp.where(c == 0, mine, theirs), jnp.where(c == 0, theirs, mine)], axis=1
    )

    outgoing = dot(placing, trunk, ((1,), (0,))).astype(BF)
    arrived = exchange(outgoing.reshape(nb, nx * cap, block), BATCH)
    tower_local = arrived.reshape(nx, slots, block).transpose(1, 0, 2).reshape(slots, width)
    after, before = shift(tower_local, "y", -1), shift(tower_local, "y", 1)
    middle = slots // 2
    beyond = [shift(after[:middle], "y", -1), shift(before[middle:], "y", 1)]
    around = [tower_local, after, jnp.concatenate(beyond, axis=0), before]
    tower, whose = [], []
    for s, piece in enumerate(around):
        tower += [piece, lax.ppermute(piece, "c", [(0, 1), (1, 0)])]
        whose += [(y + s) % ny * 2 + c, (y + s) % ny * 2 + 1 - c]

    whose = jnp.stack(whose).astype(jnp.int32)
    crossed, sent = cross_layer(
        whose,
        tower,
        weight.reshape(nm, width, width),
        back_own,
        back_other,
        cross_b,
        out_w,
        (nb, nx * cap + 16, block),
    )
    local_float = tower_local.astype(F32)

    returned = exchange(sent, BATCH)
    logit_part = jnp.sum(crossed * out_float[None, :], axis=1)
    logit_sum = logit_part.reshape(nx, slots // nx)
    logit_sum = logit_sum + lax.ppermute(logit_sum, "c", [(0, 1), (1, 0)])
    for far in (1, 2):
        logit_sum = logit_sum + lax.ppermute(logit_sum, "y", [(i, i ^ far) for i in range(ny)])

    at = lax.axis_index(BATCH)
    mask = jnp.sum(
        jnp.where(
            ids_all[:, :, None] == jnp.arange(tower_owner.shape[0], dtype=jnp.int32),
            tower_owner[None, None, :],
            0,
        ),
        axis=2,
    ) == at
    before = jnp.sum(
        (mask[:, None, :] & (place[None, :, None] > place[None, None, :])).astype(jnp.int32), axis=2
    )
    slot_labels = jnp.sum(
        jnp.where(
            mask[:, :, None] & (before[:, :, None] == jnp.arange(cap, dtype=jnp.int32)),
            labels_all[:, :, None],
            0.0,
        ),
        axis=1,
    )
    slot_labels = slot_labels.reshape(nx, nz, cap).transpose(1, 0, 2).reshape(slots)
    d_logit = jax.nn.sigmoid(logit_sum.reshape(slots)) - slot_labels
    grad_outvec = jnp.sum(d_logit[:, None] * crossed, axis=0)
    d_pre = d_logit[:, None] * out_float[None, :] * local_float
    grad_bias = jnp.sum(d_pre, axis=0)
    d_pre_b = d_pre.astype(BF)
    grad_weight = cross_grad(whose, tower, d_pre_b).reshape(1, nm * width, width)
    returned, grad_weight = lax.optimization_barrier((returned, grad_weight))

    row_cols = dot(placing_back, returned.reshape(nb * stride, block), ((0,), (0,)))
    per_row = block // (nx * cap)
    logits = returned[:, nx * cap : nx * cap + 2].reshape(nb, 2, per_row, nx * cap)
    logits = lax.dynamic_index_in_dim(logits, z % per_row, 2, False).transpose(1, 0, 2)
    logits = dot(logits.reshape(2, nb * nx * cap), placing, ((1,), (0,)))
    mixed = jnp.concatenate(
        [row_cols.astype(BF), logits.astype(BF).reshape(2 * nx, block)], axis=0
    )
    mixed = jnp.stack(ring(mixed, "y"))
    mixed = turned(jnp.stack(pair(mixed), axis=1), (ny - y) % ny)
    mixed = mixed.reshape(nm, group + 2 * nx, block)
    logit_rows = jnp.sum(mixed[:, group:].astype(F32), axis=0)
    logit_rows = logit_rows[:nx] + logit_rows[nx:]
    d_logit_rows = (jax.nn.sigmoid(logit_rows) - labels_group).reshape(group)
    by_row = d_logit_rows[:, None]
    d_rows = mixed[:, :group]

    d_hidden = jnp.einsum("mrj,mkj->rk", d_rows, down, preferred_element_type=F32)
    d_hidden = (d_hidden * by_row).astype(BF)
    d_parts = [d_hidden[:, s * block : (s + 1) * block] for s in range(nx)]
    d_hidden = d_parts[0].astype(F32)
    for s in range(1, nx):
        d_hidden = d_hidden + lax.ppermute(
            d_parts[s], "x", [(i, (i + s) % nx) for i in range(nx)]
        ).astype(F32)
    scaled_hidden = (hidden.astype(F32) * by_row).astype(BF)
    down_term = jnp.einsum("rk,mrj->mkj", scaled_hidden, d_rows, preferred_element_type=F32)
    d_up = d_hidden * activated
    d_gate = d_hidden * up_pre * gate_sig * (1.0 + gate_pre * (1.0 - gate_sig))
    d_both = jnp.concatenate([d_gate, d_up], axis=1).astype(BF).reshape(nx, rows, 2 * block)
    d_both = turned(d_both, x).reshape(group, 2 * block)
    term = dot(feats, d_both, ((0,), (0,))).astype(BF)
    down_term = down_term.astype(BF)
    term_for = lambda s: lax.dynamic_index_in_dim(down_term, (z + s) % nz, 0, False)
    far = nz // 2 - 1
    total = term_for(0).astype(F32) + shift(term_for(far + 1), "z", far + 1).astype(F32)
    forth, back = term_for(far), term_for(-far)
    for s in range(1, far):
        forth, back = shift(forth, "z", 1), shift(back, "z", -1)
        forth = (forth.astype(F32) + term_for(far - s).astype(F32)).astype(BF)
        back = (back.astype(F32) + term_for(s - far).astype(F32)).astype(BF)
    forth, back, term = lax.optimization_barrier((forth, back, term))
    grad_down = 0.0
    for piece, ahead in ((total.astype(BF), 0), (forth, 1), (back, -1)):
        owners = [
            (i * nz + k, nx * ((k + ahead) % nz) + i) for i in range(nx) for k in range(nz)
        ]
        grad_down = grad_down + lax.ppermute(piece, BATCH, owners).astype(F32)
    grad_down = grad_down.reshape(nx, block, block)
    grad_down = turned(grad_down, (nx - lax.axis_index(BATCH) % nx) % nx).reshape(width, block)
    term = exchange(term.reshape(nb, part, 2 * block), BATCH)
    term = jnp.sum(term.reshape(nx, nz, part, 2 * block).astype(F32), axis=1)
    flat = lambda t: t.transpose(1, 0, 2).reshape(part, nx * block)
    grad_gate, grad_up = flat(term[:, :, :block]), flat(term[:, :, block:])

    return (grad_gate, grad_up, grad_down, grad_weight, grad_bias[None], grad_outvec[None])


def solution(mesh):
    split = Mesh(mesh.devices.reshape(4, 2, 4, 8), ("y", "c", "x", "z"))
    placed = (
        P(BATCH, None),
        P(BATCH),
        P(BATCH, None),
        P(),
        P(BATCH, MP),
        P(BATCH, MP),
        P(MP, BATCH),
        P(BATCH, None, MP),
        P(BATCH, MP),
        P(BATCH, MP),
    )
    return jax.shard_map(
        per_device,
        mesh=split,
        in_specs=placed,
        out_specs=(
            P(BATCH, MP),
            P(BATCH, MP),
            P(MP, BATCH),
            P(BATCH, None, MP),
            P(BATCH, MP),
            P(BATCH, MP),
        ),
        check_vma=False,
    )
```
